512 devices in a mesh: section: 4 (over y_lo, core), seq: 128 (over z, x, y_hi).
Axes of the slice: x: 4, y: 4 (y_hi: 2, y_lo: 2; y = y_hi * 2 + y_lo), z: 16, core: 2. Of those that a mesh axis runs over, the one named last changes fastest.
Arguments:
- skip_rows: bfloat16 [4, 16384, 2048], P('section', 'seq'), may hold values from -6 to 6
- molecule_kv: bfloat16 [4, 2048, 4096], P('section', 'seq'), may hold values from -139 to 139
- norm_gain: float32 [2048], replicated, may hold values from 0.1 to 1.9
- sink_kv: float32 [2048], replicated, may hold values from -4 to 4
- w_query: bfloat16 [2048, 1024], replicated, may hold values from -0.125 to 0.125
Outputs:
- upsampled: bfloat16 [4, 16384, 1024], P('section', 'seq')
The draws below stay inside these ranges and needn't reach their ends.
All inputs are finite; a program needn't handle non-finite values.
Results may differ from the reference program's by a relative error of at most 0.014.
The reference program's roundings to bfloat16 on the way (of `normed`, `query`, `keyval` and `weight`) count: a program that leaves them out, or rounds other values in their place, can miss the bound.
Values may be sent and summed in bfloat16 or wider, within the bound.
No kernel may reach another device: no remote copies, remote signals or barrier semaphores. Data moves between devices by JAX's collectives and lax.ppermute only.
A program may use at most 64 MiB of HBM per device.

```python
import jax
import jax.numpy as jnp
from jax import lax

D = 2048
NH = 16
HD = 64
SHORT = 4
BACK = 3
CH_DEV = 128
HQ = 1024
MOL_DEV = 32
REACH = 96
MICRO = 4
CHARS = 16384
MOLS = 4096


def draw_molecule_kv(key, part):
    key = jax.random.fold_in(key, 11)
    key_main = jax.random.fold_in(key, 0)
    base = jax.random.truncated_normal(key_main, -4.0, 4.0, (MICRO, 2 * HQ, MOLS), jnp.float32)
    return base.astype(jnp.bfloat16)


def block_scale(own_key, dims, cuts, low, high):
    factor_of = 1.0
    for dim, blocks in cuts:
        steps = jax.random.uniform(jax.random.fold_in(jax.random.fold_in(own_key, 6), dim), (blocks,), jnp.float32, low / len(cuts), high / len(cuts))
        factor_of = factor_of * jnp.repeat(jnp.exp(steps), dims[dim] // blocks).reshape((-1,) + (1,) * (len(dims) - 1 - dim))
    return factor_of


def centred(own_key, dims, scale, bound, pieces=(), kind=jnp.bfloat16):
    level = block_scale(own_key, dims, pieces, -0.22, 0.18) if pieces else 1.0
    values = jax.random.normal(own_key, dims, jnp.float32) * scale * level
    return jnp.minimum(jnp.maximum(values, -bound), bound).astype(kind)


def setup_inputs(seed: int = 0) -> dict:
    splits = jax.random.split(jax.random.key(seed), 6)
    skip_rows = centred(splits[0], (MICRO, CHARS, D), 1.0, 6.0, ((0, 4), (1, 128)))
    molecule_kv = draw_molecule_kv(jax.random.fold_in(splits[5], 71), 0)
    norm_gain = jnp.clip(1.0 + 0.18 * jax.random.normal(splits[2], (D,), jnp.float32), 0.1, 1.9)
    sink_kv = centred(splits[3], (2 * HQ,), 1.0, 4.0, (), jnp.float32)
    w_query = centred(splits[4], (D, HQ), D ** -0.5, 0.125)
    return dict(skip_rows=skip_rows, molecule_kv=molecule_kv, norm_gain=norm_gain, sink_kv=sink_kv, w_query=w_query)


def norm_rows(rows, gain):
    values = rows.astype(jnp.float32)
    inverse = lax.rsqrt(lax.optimization_barrier(jnp.mean(values * values, axis=-1, keepdims=True)) + 1e-06)
    return (values * inverse * gain).astype(jnp.bfloat16)

def attend(query, keyval, sink_kv, block_index):
    chars = query.shape[0]
    width = keyval.shape[1]
    query_heads = query.reshape(chars, NH, HD).astype(jnp.float32)
    keys = keyval[:HQ].reshape(NH, HD, width).astype(jnp.float32)
    values = keyval[HQ:].reshape(NH, HD, width).astype(jnp.float32)
    sink_key = sink_kv[:HQ].reshape(NH, HD)
    sink_value = sink_kv[HQ:].reshape(NH, HD)
    scores = jnp.einsum('qhd,hdk->hqk', query_heads, keys, precision=lax.Precision.HIGHEST) * 0.125
    sink = lax.optimization_barrier(jnp.sum(query_heads * sink_key[None], axis=-1)).T * 0.125
    place = block_index * chars + jnp.arange(chars, dtype=jnp.int32)
    molecule = (block_index - BACK) * MOL_DEV + jnp.arange(width, dtype=jnp.int32)
    lag = place[:, None] - SHORT * molecule[None, :] - (SHORT - 1)
    visible = (molecule[None, :] >= 0) & (lag >= 0) & (lag < SHORT * REACH)
    scores = jnp.where(visible[None], scores, jnp.float32(-1e+30))
    top = jnp.maximum(lax.optimization_barrier(jnp.max(scores, axis=-1)), sink)
    expo = jnp.exp(scores - top[..., None])
    sink_expo = jnp.exp(sink - top)
    total = lax.optimization_barrier(jnp.sum(expo, axis=-1)) + sink_expo
    weight = (expo / total[..., None]).astype(jnp.bfloat16)
    sink_weight = (sink_expo / total).astype(jnp.bfloat16)
    mixed = jnp.einsum('hqk,hdk->qhd', weight.astype(jnp.float32), values, precision=lax.Precision.HIGHEST)
    mixed = mixed + sink_weight.T[..., None].astype(jnp.float32) * sink_value[None]
    return mixed.reshape(chars, HQ).astype(jnp.bfloat16)

def one_batch(skip_block, kv_block, norm_gain, sink_kv, w_query):
    normed = norm_rows(skip_block, norm_gain)
    query = jnp.dot(normed, w_query, preferred_element_type=jnp.float32).astype(jnp.bfloat16)
    padded = jnp.concatenate([jnp.zeros((2 * HQ, BACK * MOL_DEV), jnp.bfloat16), kv_block], axis=1)

    def block(index):
        query_rows = lax.dynamic_slice_in_dim(query, (index * CH_DEV).astype(jnp.int32), CH_DEV, 0)
        keyval = lax.dynamic_slice_in_dim(padded, (index * MOL_DEV).astype(jnp.int32), (BACK + 1) * MOL_DEV, 1)
        return attend(query_rows, keyval, sink_kv, index)
    blocks = lax.map(block, jnp.arange(CHARS // CH_DEV, dtype=jnp.int32))
    return blocks.reshape(CHARS, HQ)

def reference(skip_rows, molecule_kv, norm_gain, sink_kv, w_query):
    results = [one_batch(skip_rows[b], molecule_kv[(b - 1) % MICRO], norm_gain, sink_kv, w_query) for b in range(MICRO)]
    return jnp.stack(results, axis=0)
```

```python
import functools

import jax
import jax.numpy as jnp
from jax import lax
from jax.experimental import pallas as pl
from jax.experimental.pallas import tpu as pltpu
from jax.sharding import PartitionSpec as P

NH = 16
HD = 64
SHORT = 4
BACK = 3
HQ = 1024
LANES = 128
PLANE = 8
ROWS = 16
VMEM = pl.BlockSpec(memory_space=pltpu.VMEM)
SMALL = pltpu.CompilerParams(vmem_limit_bytes=16 * 1024 * 1024)


def norm_rows(rows, gain):
    values = rows.astype(jnp.float32)
    inverse = lax.rsqrt(jnp.mean(values * values, axis=-1, keepdims=True) + 1e-06)
    return (values * inverse * gain).astype(jnp.bfloat16)


def spread_kernel(kv_ref, out_ref):
    planes, _, wide = out_ref.shape
    step = kv_ref.shape[1] // planes
    for c in range(planes):
        first = c * step - (wide - step)
        if first < 0:
            out_ref[c, :, : wide - step] = jnp.zeros((ROWS, wide - step), jnp.bfloat16)
            out_ref[c, :, wide - step :] = kv_ref[:, :step]
        else:
            out_ref[c] = kv_ref[:, first : first + wide]


def window_kernel(in_ref, out_ref):
    rows = in_ref.shape[0] * in_ref.shape[1]
    data = in_ref[...].reshape(rows, in_ref.shape[2])
    for w in range(PLANE):
        first = 32 * w + 32
        out_ref[w] = data[:, first : first + LANES]


def attend_kernel(q_ref, kv_ref, sink_ref, value_ref, out_ref):
    chars = q_ref.shape[0]
    block = lax.axis_index("seq")
    char = lax.broadcasted_iota(jnp.int32, (chars, 2 * LANES), 0)
    slot = lax.rem(lax.broadcasted_iota(jnp.int32, (chars, 2 * LANES), 1), LANES)
    lag = char - SHORT * slot + (SHORT * BACK * 32 - (SHORT - 1))
    visible = (lag >= 0) & (lag < SHORT * BACK * 32) & (slot >= (BACK - block) * 32)
    zero = jnp.zeros((HD, LANES), jnp.bfloat16)
    left = lax.broadcasted_iota(jnp.int32, (chars, LANES), 1) < HD

    def pair(first):
        parts = [kv_ref[w, first : first + ROWS, :] for w in range(PLANE)]
        even = jnp.concatenate(parts[: PLANE // 2], axis=0)
        odd = jnp.concatenate(parts[PLANE // 2 :], axis=0)
        return jnp.concatenate(
            [jnp.concatenate([even, zero], axis=1), jnp.concatenate([zero, odd], axis=1)], axis=0
        )

    for m in range(NH // 2):
        lanes = slice(m * LANES, (m + 1) * LANES)
        scores = jnp.dot(q_ref[:, lanes], pair(m * ROWS), preferred_element_type=jnp.float32)
        scores = jnp.where(visible, scores * 0.125, jnp.float32(-1e30))
        weights, sinks = [], []
        for side in range(2):
            score = scores[:, side * LANES : (side + 1) * LANES]
            sink = sink_ref[:, 2 * m + side : 2 * m + side + 1]
            top = jnp.maximum(jnp.max(score, axis=-1, keepdims=True), sink)
            expo = jnp.exp(score - top)
            sink_expo = jnp.exp(sink - top)
            total = jnp.sum(expo, axis=-1, keepdims=True) + sink_expo
            weights.append((expo / total).astype(jnp.bfloat16))
            sinks.append((sink_expo / total).astype(jnp.bfloat16).astype(jnp.float32))
        mixed = lax.dot_general(
            jnp.concatenate(weights, axis=1),
            pair((m + NH // 2) * ROWS),
            (((1,), (1,)), ((), ())),
            preferred_element_type=jnp.float32,
        )
        mixed = mixed + jnp.where(left, sinks[0], sinks[1]) * value_ref[:, lanes]
        out_ref[:, lanes] = mixed.astype(jnp.bfloat16)


def shards(skip_rows, molecule_kv, norm_gain, sink_kv, w_query):
    seq = lax.axis_size("seq")
    sections = lax.axis_size("section")
    planes = seq // PLANE
    columns = [[z * PLANE + w for z in range(planes)] for w in range(PLANE)]
    rows = [[z * PLANE + w for w in range(PLANE)] for z in range(planes)]
    width = molecule_kv.shape[2] // planes

    arrived = lax.ppermute(
        molecule_kv, "section", [((i - 1) % sections, i) for i in range(sections)]
    )[0]
    normed = norm_rows(skip_rows[0], norm_gain)
    query = jnp.dot(normed, w_query, preferred_element_type=jnp.float32).astype(jnp.bfloat16)
    chars = query.shape[0]
    sink_key = sink_kv[:HQ].reshape(NH, HD)
    sink = jnp.sum(query.astype(jnp.float32).reshape(chars, NH, HD) * sink_key[None], axis=-1)
    sink = sink * 0.125

    chunks = pl.pallas_call(
        spread_kernel,
        out_shape=jax.ShapeDtypeStruct((planes, ROWS, width + LANES), jnp.bfloat16),
        in_specs=[VMEM],
        out_specs=VMEM,
        compiler_params=SMALL,
    )(arrived)
    chunks = lax.all_to_all(chunks, "seq", 0, 0, axis_index_groups=columns, tiled=True)
    windows = pl.pallas_call(
        window_kernel,
        out_shape=jax.ShapeDtypeStruct((PLANE, planes * ROWS, LANES), jnp.bfloat16),
        in_specs=[VMEM],
        out_specs=VMEM,
        compiler_params=SMALL,
    )(chunks)
    keyval = lax.all_to_all(windows, "seq", 0, 0, axis_index_groups=rows, tiled=True)
    mixed = pl.pallas_call(
        attend_kernel,
        out_shape=jax.ShapeDtypeStruct((chars, HQ), jnp.bfloat16),
        in_specs=[VMEM] * 4,
        out_specs=VMEM,
        compiler_params=SMALL,
    )(query, keyval, sink, sink_kv[HQ:][None])
    return mixed[None]


def solution(mesh):
    return jax.shard_map(
        shards,
        mesh=mesh,
        in_specs=(P("section", "seq", None), P("section", "seq", None), P(), P(), P()),
        out_specs=P("section", "seq", None),
        check_vma=False,
    )
```

```python
import functools

import jax
import jax.numpy as jnp
from jax import lax
from jax.experimental import pallas as pl
from jax.experimental.pallas import tpu as pltpu
from jax.sharding import PartitionSpec as P

NH = 16
HD = 64
SHORT = 4
BACK = 3
HQ = 1024
LANES = 128
PLANE = 8
ROWS = 16
VMEM = pl.BlockSpec(memory_space=pltpu.VMEM)
SMALL = pltpu.CompilerParams(vmem_limit_bytes=16 * 1024 * 1024)


def norm_rows(rows, gain):
    values = rows.astype(jnp.float32)
    inverse = lax.rsqrt(jnp.mean(values * values, axis=-1, keepdims=True) + 1e-06)
    return (values * inverse * gain).astype(jnp.bfloat16)


def spread_kernel(kv_ref, out_ref):
    planes, _, wide = out_ref.shape
    step = kv_ref.shape[1] // planes
    for c in range(planes):
        first = c * step - (wide - step)
        if first < 0:
            out_ref[c, :, : wide - step] = jnp.zeros((ROWS, wide - step), jnp.bfloat16)
            out_ref[c, :, wide - step :] = kv_ref[:, :step]
        else:
            out_ref[c] = kv_ref[:, first : first + wide]


def window_kernel(in_ref, out_ref):
    rows = in_ref.shape[0] * in_ref.shape[1]
    data = in_ref[...].reshape(rows, in_ref.shape[2])
    for w in range(PLANE):
        first = 32 * w + 32
        out_ref[w] = data[:, first : first + LANES]


def attend_kernel(q_ref, kv_ref, sink_ref, value_ref, out_ref):
    chars = q_ref.shape[1]
    block = lax.axis_index("seq")
    char = lax.broadcasted_iota(jnp.int32, (LANES, chars), 1)
    slot = lax.broadcasted_iota(jnp.int32, (LANES, chars), 0)
    lag = char - SHORT * slot + (SHORT * BACK * 32 - (SHORT - 1))
    visible = (lag >= 0) & (lag < SHORT * BACK * 32) & (slot >= (BACK - block) * 32)
    hidden = jnp.where(visible, jnp.float32(0.0), jnp.float32(-1e30))
    zero = jnp.zeros((HD, chars), jnp.bfloat16)

    def pair(first):
        return jnp.concatenate([kv_ref[w, first : first + ROWS, :] for w in range(PLANE)], axis=0)

    for m in range(NH // 2):
        rows = slice(m * LANES, (m + 1) * LANES)
        query = q_ref[rows, :]
        query = jnp.concatenate(
            [
                jnp.concatenate([query[:HD], zero], axis=0),
                jnp.concatenate([zero, query[HD:]], axis=0),
            ],
            axis=1,
        )
        scores = lax.dot_general(
            pair(m * ROWS), query, (((0,), (0,)), ((), ())), preferred_element_type=jnp.float32
        )
        weights, sinks = [], []
        for side in range(2):
            score = scores[:, side * chars : (side + 1) * chars] * 0.125 + hidden
            sink = sink_ref[2 * m + side : 2 * m + side + 1, :]
            top = jnp.maximum(jnp.max(score, axis=0, keepdims=True), sink)
            expo = jnp.exp(score - top)
            sink_expo = jnp.exp(sink - top)
            inverse = 1.0 / (jnp.sum(expo, axis=0, keepdims=True) + sink_expo)
            weights.append((expo * inverse).astype(jnp.bfloat16))
            sinks.append((sink_expo * inverse).astype(jnp.bfloat16).astype(jnp.float32))
        mixed = jnp.dot(
            pair((m + NH // 2) * ROWS),
            jnp.concatenate(weights, axis=1),
            preferred_element_type=jnp.float32,
        )
        value = value_ref[rows, :]
        even = mixed[:HD, :chars] + sinks[0] * value[:HD]
        odd = mixed[HD:, chars:] + sinks[1] * value[HD:]
        mixed = jnp.concatenate([even, odd], axis=0)
        out_ref[:, rows] = mixed.T.astype(jnp.bfloat16)


def shards(skip_rows, molecule_kv, norm_gain, sink_kv, w_query):
    seq = lax.axis_size("seq")
    sections = lax.axis_size("section")
    planes = seq // PLANE
    columns = [[z * PLANE + w for z in range(planes)] for w in range(PLANE)]
    rows = [[z * PLANE + w for w in range(PLANE)] for z in range(planes)]
    width = molecule_kv.shape[2] // planes

    arrived = lax.ppermute(
        molecule_kv, "section", [((i - 1) % sections, i) for i in range(sections)]
    )[0]
    normed = norm_rows(skip_rows[0], norm_gain)
    query = jnp.dot(normed, w_query, preferred_element_type=jnp.float32).astype(jnp.bfloat16)
    chars = query.shape[0]
    turned = query.T
    sink = turned.astype(jnp.float32).reshape(NH, HD, chars) * sink_kv[:HQ].reshape(NH, HD, 1)
    sink = jnp.sum(sink, axis=1) * 0.125
    sink_value = jnp.broadcast_to(sink_kv[HQ:, None], (HQ, chars))

    chunks = pl.pallas_call(
        spread_kernel,
        out_shape=jax.ShapeDtypeStruct((planes, ROWS, width + LANES), jnp.bfloat16),
        in_specs=[VMEM],
        out_specs=VMEM,
        compiler_params=SMALL,
    )(arrived)
    chunks = lax.all_to_all(chunks, "seq", 0, 0, axis_index_groups=columns, tiled=True)
    chunks, turned, sink, sink_value = lax.optimization_barrier((chunks, turned, sink, sink_value))
    windows = pl.pallas_call(
        window_kernel,
        out_shape=jax.ShapeDtypeStruct((PLANE, planes * ROWS, LANES), jnp.bfloat16),
        in_specs=[VMEM],
        out_specs=VMEM,
        compiler_params=SMALL,
    )(chunks)
    keyval = lax.all_to_all(windows, "seq", 0, 0, axis_index_groups=rows, tiled=True)
    mixed = pl.pallas_call(
        attend_kernel,
        out_shape=jax.ShapeDtypeStruct((chars, HQ), jnp.bfloat16),
        in_specs=[VMEM] * 4,
        out_specs=VMEM,
        compiler_params=SMALL,
    )(turned, keyval, sink, sink_value)
    return mixed[None]


def solution(mesh):
    return jax.shard_map(
        shards,
        mesh=mesh,
        in_specs=(P("section", "seq", None), P("section", "seq", None), P(), P(), P()),
        out_specs=P("section", "seq", None),
        check_vma=False,
    )
```

```python
import functools

import jax
import jax.numpy as jnp
from jax import lax
from jax.experimental import pallas as pl
from jax.experimental.pallas import tpu as pltpu
from jax.sharding import PartitionSpec as P

NH = 16
HD = 64
SHORT = 4
BACK = 3
HQ = 1024
LANES = 128
PLANE = 8
PLACES = (5, 4, 7, 6, 1, 0, 3, 2)
ROWS = 16
VMEM = pl.BlockSpec(memory_space=pltpu.VMEM)
SMALL = pltpu.CompilerParams(vmem_limit_bytes=16 * 1024 * 1024)


def plane_order(planes):
    bits = planes.bit_length() - 1
    turned = [int(format(i, "b").zfill(bits)[::-1], 2) for i in range(planes)]
    return tuple((i + planes * 11 // 16) % planes for i in turned)


def norm_rows(rows, gain):
    values = rows.astype(jnp.float32)
    inverse = lax.rsqrt(jnp.mean(values * values, axis=-1, keepdims=True) + 1e-06)
    return (values * inverse * gain).astype(jnp.bfloat16)


def spread_kernel(order, kv_ref, out_ref):
    planes, _, wide = out_ref.shape
    step = kv_ref.shape[1] // planes
    for c, plane in enumerate(order):
        first = plane * step - (wide - step)
        if first < 0:
            out_ref[c, :, : wide - step] = jnp.zeros((ROWS, wide - step), jnp.bfloat16)
            out_ref[c, :, wide - step :] = kv_ref[:, :step]
        else:
            out_ref[c] = kv_ref[:, first : first + wide]


def window_kernel(in_ref, out_ref):
    rows = in_ref.shape[0] * in_ref.shape[1]
    data = in_ref[...].reshape(rows, in_ref.shape[2])
    for j, w in enumerate(PLACES):
        first = 32 * w + 32
        out_ref[j] = data[:, first : first + LANES]


def attend_kernel(order, q_ref, kv_ref, sink_ref, value_ref, out_ref):
    chars = q_ref.shape[1]
    block = lax.axis_index("seq")
    char = lax.broadcasted_iota(jnp.int32, (LANES, chars), 1)
    slot = lax.broadcasted_iota(jnp.int32, (LANES, chars), 0)
    lag = char - SHORT * slot + (SHORT * BACK * 32 - (SHORT - 1))
    visible = (lag >= 0) & (lag < SHORT * BACK * 32) & (slot >= (BACK - block) * 32)
    hidden = jnp.where(visible, jnp.float32(0.0), jnp.float32(-1e30))
    zero = jnp.zeros((HD, chars), jnp.bfloat16)

    def pair(plane):
        first = order.index(plane) * ROWS
        return jnp.concatenate([kv_ref[PLACES.index(w), first : first + ROWS, :] for w in range(PLANE)], axis=0)

    for m in range(NH // 2):
        rows = slice(m * LANES, (m + 1) * LANES)
        query = q_ref[rows, :]
        query = jnp.concatenate(
            [
                jnp.concatenate([query[:HD], zero], axis=0),
                jnp.concatenate([zero, query[HD:]], axis=0),
            ],
            axis=1,
        )
        scores = lax.dot_general(
            pair(m), query, (((0,), (0,)), ((), ())), preferred_element_type=jnp.float32
        )
        weights, sinks = [], []
        for side in range(2):
            score = scores[:, side * chars : (side + 1) * chars] * 0.125 + hidden
            sink = sink_ref[2 * m + side : 2 * m + side + 1, :]
            top = jnp.maximum(jnp.max(score, axis=0, keepdims=True), sink)
            expo = jnp.exp(score - top)
            sink_expo = jnp.exp(sink - top)
            inverse = 1.0 / (jnp.sum(expo, axis=0, keepdims=True) + sink_expo)
            weights.append((expo * inverse).astype(jnp.bfloat16))
            sinks.append((sink_expo * inverse).astype(jnp.bfloat16).astype(jnp.float32))
        mixed = jnp.dot(
            pair(m + NH // 2),
            jnp.concatenate(weights, axis=1),
            preferred_element_type=jnp.float32,
        )
        value = value_ref[rows, :]
        even = mixed[:HD, :chars] + sinks[0] * value[:HD]
        odd = mixed[HD:, chars:] + sinks[1] * value[HD:]
        mixed = jnp.concatenate([even, odd], axis=0)
        out_ref[:, rows] = mixed.T.astype(jnp.bfloat16)


def shards(skip_rows, molecule_kv, norm_gain, sink_kv, w_query):
    seq = lax.axis_size("seq")
    sections = lax.axis_size("section")
    planes = seq // PLANE
    order = plane_order(planes)
    columns = [[z * PLANE + w for z in order] for w in range(PLANE)]
    rows = [[z * PLANE + w for w in PLACES] for z in range(planes)]
    width = molecule_kv.shape[2] // planes

    arrived = lax.ppermute(
        molecule_kv, "section", [((i - 1) % sections, i) for i in range(sections)]
    )[0]
    normed = norm_rows(skip_rows[0], norm_gain)
    query = jnp.dot(normed, w_query, preferred_element_type=jnp.float32).astype(jnp.bfloat16)
    chars = query.shape[0]
    turned = query.T
    sink = turned.astype(jnp.float32).reshape(NH, HD, chars) * sink_kv[:HQ].reshape(NH, HD, 1)
    sink = jnp.sum(sink, axis=1) * 0.125
    sink_value = jnp.broadcast_to(sink_kv[HQ:, None], (HQ, chars))

    chunks = pl.pallas_call(
        functools.partial(spread_kernel, order),
        out_shape=jax.ShapeDtypeStruct((planes, ROWS, width + LANES), jnp.bfloat16),
        in_specs=[VMEM],
        out_specs=VMEM,
        compiler_params=SMALL,
    )(arrived)
    chunks = lax.all_to_all(chunks, "seq", 0, 0, axis_index_groups=columns, tiled=True)
    chunks, turned, sink, sink_value = lax.optimization_barrier((chunks, turned, sink, sink_value))
    windows = pl.pallas_call(
        window_kernel,
        out_shape=jax.ShapeDtypeStruct((PLANE, planes * ROWS, LANES), jnp.bfloat16),
        in_specs=[VMEM],
        out_specs=VMEM,
        compiler_params=SMALL,
    )(chunks)
    keyval = lax.all_to_all(windows, "seq", 0, 0, axis_index_groups=rows, tiled=True)
    mixed = pl.pallas_call(
        functools.partial(attend_kernel, order),
        out_shape=jax.ShapeDtypeStruct((chars, HQ), jnp.bfloat16),
        in_specs=[VMEM] * 4,
        out_specs=VMEM,
        compiler_params=SMALL,
    )(turned, keyval, sink, sink_value)
    return mixed[None]


def solution(mesh):
    return jax.shard_map(
        shards,
        mesh=mesh,
        in_specs=(P("section", "seq", None), P("section", "seq", None), P(), P(), P()),
        out_specs=P("section", "seq", None),
        check_vma=False,
    )
```

```python
import functools

import jax
import jax.numpy as jnp
from jax import lax
from jax.experimental import pallas as pl
from jax.experimental.pallas import tpu as pltpu
from jax.sharding import PartitionSpec as P

NH = 16
HD = 64
SHORT = 4
BACK = 3
HQ = 1024
LANES = 128
PLANE = 8
FOLD = 2
PLANE_PLACES = (5, 4, 7, 6, 1, 0, 3, 2)
PLACES = tuple(p for w in PLANE_PLACES for p in (PLANE + w, w))
ROWS = 16
VMEM = pl.BlockSpec(memory_space=pltpu.VMEM)
SMALL = pltpu.CompilerParams(vmem_limit_bytes=16 * 1024 * 1024)


def part_order(parts):
    bits = parts.bit_length() - 1
    turned = [int(format(i, "b").zfill(bits)[::-1], 2) for i in range(parts)]
    return tuple((i + parts * 5 // 8) % parts for i in turned)


def norm_rows(rows, gain):
    values = rows.astype(jnp.float32)
    inverse = lax.rsqrt(jnp.mean(values * values, axis=-1, keepdims=True) + 1e-06)
    return (values * inverse * gain).astype(jnp.bfloat16)


def spread_kernel(order, kv_ref, out_ref):
    parts, _, wide = out_ref.shape
    step = kv_ref.shape[1] // parts
    for c, part in enumerate(order):
        first = part * step - (wide - step)
        if first < 0:
            out_ref[c, :, : wide - step] = jnp.zeros((ROWS, wide - step), jnp.bfloat16)
            out_ref[c, :, wide - step :] = kv_ref[:, :step]
        else:
            out_ref[c] = kv_ref[:, first : first + wide]


def window_kernel(in_ref, out_ref):
    rows = in_ref.shape[0] * in_ref.shape[1]
    data = in_ref[...].reshape(rows, in_ref.shape[2])
    for j, w in enumerate(PLACES):
        first = 32 * w + 32
        out_ref[j] = data[:, first : first + LANES]


def attend_kernel(order, q_ref, kv_ref, sink_ref, value_ref, out_ref):
    chars = q_ref.shape[1]
    block = lax.axis_index("seq")
    char = lax.broadcasted_iota(jnp.int32, (LANES, chars), 1)
    slot = lax.broadcasted_iota(jnp.int32, (LANES, chars), 0)
    lag = char - SHORT * slot + (SHORT * BACK * 32 - (SHORT - 1))
    visible = (lag >= 0) & (lag < SHORT * BACK * 32) & (slot >= (BACK - block) * 32)
    hidden = jnp.where(visible, jnp.float32(0.0), jnp.float32(-1e30))
    zero = jnp.zeros((HD, chars), jnp.bfloat16)

    def pair(plane):
        first = order.index(plane // FOLD) * ROWS
        slots = [PLACES.index(plane % FOLD * PLANE + w) for w in range(PLANE)]
        return jnp.concatenate([kv_ref[s, first : first + ROWS, :] for s in slots], axis=0)

    for m in range(NH // 2):
        rows = slice(m * LANES, (m + 1) * LANES)
        query = q_ref[rows, :]
        query = jnp.concatenate(
            [
                jnp.concatenate([query[:HD], zero], axis=0),
                jnp.concatenate([zero, query[HD:]], axis=0),
            ],
            axis=1,
        )
        scores = lax.dot_general(
            pair(m), query, (((0,), (0,)), ((), ())), preferred_element_type=jnp.float32
        )
        weights, sinks = [], []
        for side in range(2):
            score = scores[:, side * chars : (side + 1) * chars] * 0.125 + hidden
            sink = sink_ref[2 * m + side : 2 * m + side + 1, :]
            top = jnp.maximum(jnp.max(score, axis=0, keepdims=True), sink)
            expo = jnp.exp(score - top)
            sink_expo = jnp.exp(sink - top)
            inverse = 1.0 / (jnp.sum(expo, axis=0, keepdims=True) + sink_expo)
            weights.append((expo * inverse).astype(jnp.bfloat16))
            sinks.append((sink_expo * inverse).astype(jnp.bfloat16).astype(jnp.float32))
        mixed = jnp.dot(
            pair(m + NH // 2),
            jnp.concatenate(weights, axis=1),
            preferred_element_type=jnp.float32,
        )
        value = value_ref[rows, :]
        even = mixed[:HD, :chars] + sinks[0] * value[:HD]
        odd = mixed[HD:, chars:] + sinks[1] * value[HD:]
        mixed = jnp.concatenate([even, odd], axis=0)
        out_ref[:, rows] = mixed.T.astype(jnp.bfloat16)


def shards(skip_rows, molecule_kv, norm_gain, sink_kv, w_query):
    seq = lax.axis_size("seq")
    sections = lax.axis_size("section")
    planes = seq // PLANE
    order = part_order(planes // FOLD)
    parts = planes // FOLD
    stride = FOLD * PLANE
    columns = [[z * stride + w for z in order] for w in range(stride)]
    rows = [[z * stride + w for w in PLACES] for z in range(parts)]
    width = molecule_kv.shape[2] // parts

    arrived = lax.ppermute(
        molecule_kv, "section", [((i - 1) % sections, i) for i in range(sections)]
    )[0]
    normed = norm_rows(skip_rows[0], norm_gain)
    query = jnp.dot(normed, w_query, preferred_element_type=jnp.float32).astype(jnp.bfloat16)
    chars = query.shape[0]
    turned = query.T
    sink = turned.astype(jnp.float32).reshape(NH, HD, chars) * sink_kv[:HQ].reshape(NH, HD, 1)
    sink = jnp.sum(sink, axis=1) * 0.125
    sink_value = jnp.broadcast_to(sink_kv[HQ:, None], (HQ, chars))

    chunks = pl.pallas_call(
        functools.partial(spread_kernel, order),
        out_shape=jax.ShapeDtypeStruct((parts, ROWS, width + LANES), jnp.bfloat16),
        in_specs=[VMEM],
        out_specs=VMEM,
        compiler_params=SMALL,
    )(arrived)
    chunks = lax.all_to_all(chunks, "seq", 0, 0, axis_index_groups=columns, tiled=True)
    chunks, turned, sink, sink_value = lax.optimization_barrier((chunks, turned, sink, sink_value))
    windows = pl.pallas_call(
        window_kernel,
        out_shape=jax.ShapeDtypeStruct((stride, parts * ROWS, LANES), jnp.bfloat16),
        in_specs=[VMEM],
        out_specs=VMEM,
        compiler_params=SMALL,
    )(chunks)
    keyval = lax.all_to_all(windows, "seq", 0, 0, axis_index_groups=rows, tiled=True)
    mixed = pl.pallas_call(
        functools.partial(attend_kernel, order),
        out_shape=jax.ShapeDtypeStruct((chars, HQ), jnp.bfloat16),
        in_specs=[VMEM] * 4,
        out_specs=VMEM,
        compiler_params=SMALL,
    )(turned, keyval, sink, sink_value)
    return mixed[None]


def solution(mesh):
    return jax.shard_map(
        shards,
        mesh=mesh,
        in_specs=(P("section", "seq", None), P("section", "seq", None), P(), P(), P()),
        out_specs=P("section", "seq", None),
        check_vma=False,
    )
```

```python
import functools

import jax
import jax.numpy as jnp
from jax import lax
from jax.experimental import pallas as pl
from jax.experimental.pallas import tpu as pltpu
from jax.sharding import PartitionSpec as P

NH = 16
HD = 64
SHORT = 4
BACK = 3
HQ = 1024
LANES = 128
PLANE = 8
FOLD = 2
PLACES = (13, 5, 15, 7, 12, 4, 14, 6, 11, 3, 9, 1, 10, 2, 8, 0)
ROWS = 16
VMEM = pl.BlockSpec(memory_space=pltpu.VMEM)
SMALL = pltpu.CompilerParams(vmem_limit_bytes=16 * 1024 * 1024)


def part_order(parts):
    bits = parts.bit_length() - 1
    turned = [int(format(i, "b").zfill(bits)[::-1], 2) for i in range(parts)]
    return tuple((i + parts * 5 // 8) % parts for i in turned)


def spread_kernel(order, kv_ref, out_ref):
    parts, _, wide = out_ref.shape
    step = kv_ref.shape[1] // parts
    for c, part in enumerate(order):
        first = part * step - (wide - step)
        if first < 0:
            out_ref[c, :, : wide - step] = jnp.zeros((ROWS, wide - step), jnp.bfloat16)
            out_ref[c, :, wide - step :] = kv_ref[:, :step]
        else:
            out_ref[c] = kv_ref[:, first : first + wide]


def window_kernel(in_ref, out_ref):
    rows = in_ref.shape[0] * in_ref.shape[1]
    data = in_ref[...].reshape(rows, in_ref.shape[2])
    for j, w in enumerate(PLACES):
        first = 32 * w + 32
        out_ref[j] = data[:, first : first + LANES]


def attend_kernel(order, q_ref, kv_ref, sink_ref, value_ref, out_ref):
    chars = q_ref.shape[1]
    block = lax.axis_index("seq")
    char = lax.broadcasted_iota(jnp.int32, (LANES, chars), 1)
    slot = lax.broadcasted_iota(jnp.int32, (LANES, chars), 0)
    lag = char - SHORT * slot + (SHORT * BACK * 32 - (SHORT - 1))
    visible = (lag >= 0) & (lag < SHORT * BACK * 32) & (slot >= (BACK - block) * 32)
    hidden = jnp.where(visible, jnp.float32(0.0), jnp.float32(-1e30))
    zero = jnp.zeros((HD, chars), jnp.bfloat16)

    def pair(plane):
        first = order.index(plane // FOLD) * ROWS
        slots = [PLACES.index(plane % FOLD * PLANE + w) for w in range(PLANE)]
        return jnp.concatenate([kv_ref[s, first : first + ROWS, :] for s in slots], axis=0)

    for m in range(NH // 2):
        rows = slice(m * LANES, (m + 1) * LANES)
        query = q_ref[rows, :]
        query = jnp.concatenate(
            [
                jnp.concatenate([query[:HD], zero], axis=0),
                jnp.concatenate([zero, query[HD:]], axis=0),
            ],
            axis=1,
        )
        scores = lax.dot_general(
            pair(m), query, (((0,), (0,)), ((), ())), preferred_element_type=jnp.float32
        )
        weights, sinks = [], []
        for side in range(2):
            score = scores[:, side * chars : (side + 1) * chars] * 0.125 + hidden
            sink = sink_ref[2 * m + side : 2 * m + side + 1, :]
            top = jnp.maximum(jnp.max(score, axis=0, keepdims=True), sink)
            expo = jnp.exp(score - top)
            sink_expo = jnp.exp(sink - top)
            inverse = 1.0 / (jnp.sum(expo, axis=0, keepdims=True) + sink_expo)
            weights.append((expo * inverse).astype(jnp.bfloat16))
            sinks.append((sink_expo * inverse).astype(jnp.bfloat16).astype(jnp.float32))
        mixed = jnp.dot(
            pair(m + NH // 2),
            jnp.concatenate(weights, axis=1),
            preferred_element_type=jnp.float32,
        )
        value = value_ref[rows, :]
        even = mixed[:HD, :chars] + sinks[0] * value[:HD]
        odd = mixed[HD:, chars:] + sinks[1] * value[HD:]
        mixed = jnp.concatenate([even, odd], axis=0)
        out_ref[:, rows] = mixed.T.astype(jnp.bfloat16)


def shards(skip_rows, molecule_kv, norm_gain, sink_kv, w_query):
    seq = lax.axis_size("seq")
    sections = lax.axis_size("section")
    planes = seq // PLANE
    order = part_order(planes // FOLD)
    parts = planes // FOLD
    stride = FOLD * PLANE
    columns = [[z * stride + w for z in order] for w in range(stride)]
    rows = [[z * stride + w for w in PLACES] for z in range(parts)]
    width = molecule_kv.shape[2] // parts

    arrived = lax.ppermute(
        molecule_kv, "section", [((i - 1) % sections, i) for i in range(sections)]
    )[0]
    values = skip_rows[0].astype(jnp.float32)
    inverse = lax.rsqrt(jnp.mean(values * values, axis=-1, keepdims=True) + 1e-06)
    chars = values.shape[0]
    sink_value = jnp.broadcast_to(sink_kv[HQ:, None], (HQ, chars))
    arrived, inverse, sink_value = lax.optimization_barrier((arrived, inverse, sink_value))
    normed = (values * inverse * norm_gain).astype(jnp.bfloat16)
    query = jnp.dot(normed, w_query, preferred_element_type=jnp.float32).astype(jnp.bfloat16)
    turned = query.T
    sink = turned.astype(jnp.float32).reshape(NH, HD, chars) * sink_kv[:HQ].reshape(NH, HD, 1)
    sink = jnp.sum(sink, axis=1) * 0.125

    chunks = pl.pallas_call(
        functools.partial(spread_kernel, order),
        out_shape=jax.ShapeDtypeStruct((parts, ROWS, width + LANES), jnp.bfloat16),
        in_specs=[VMEM],
        out_specs=VMEM,
        compiler_params=SMALL,
    )(arrived)
    chunks = lax.all_to_all(chunks, "seq", 0, 0, axis_index_groups=columns, tiled=True)
    chunks, turned, sink = lax.optimization_barrier((chunks, turned, sink))
    windows = pl.pallas_call(
        window_kernel,
        out_shape=jax.ShapeDtypeStruct((stride, parts * ROWS, LANES), jnp.bfloat16),
        in_specs=[VMEM],
        out_specs=VMEM,
        compiler_params=SMALL,
    )(chunks)
    keyval = lax.all_to_all(windows, "seq", 0, 0, axis_index_groups=rows, tiled=True)
    mixed = pl.pallas_call(
        functools.partial(attend_kernel, order),
        out_shape=jax.ShapeDtypeStruct((chars, HQ), jnp.bfloat16),
        in_specs=[VMEM] * 4,
        out_specs=VMEM,
        compiler_params=SMALL,
    )(turned, keyval, sink, sink_value)
    return mixed[None]


def solution(mesh):
    return jax.shard_map(
        shards,
        mesh=mesh,
        in_specs=(P("section", "seq", None), P("section", "seq", None), P(), P(), P()),
        out_specs=P("section", "seq", None),
        check_vma=False,
    )
```

```python
import functools

import jax
import jax.numpy as jnp
from jax import lax
from jax.experimental import pallas as pl
from jax.experimental.pallas import tpu as pltpu
from jax.sharding import PartitionSpec as P

NH = 16
HD = 64
SHORT = 4
BACK = 3
HQ = 1024
LANES = 128
PLANE = 8
FOLD = 2
PLACES = (13, 5, 15, 7, 12, 4, 14, 6, 11, 3, 9, 1, 10, 2, 8, 0)
ROWS = 16
VMEM = pl.BlockSpec(memory_space=pltpu.VMEM)
ANY = pl.BlockSpec(memory_space=pl.ANY)
SMALL = pltpu.CompilerParams(vmem_limit_bytes=16 * 1024 * 1024)


def part_order(parts):
    bits = parts.bit_length() - 1
    turned = [int(format(i, "b").zfill(bits)[::-1], 2) for i in range(parts)]
    return tuple((i + parts * 5 // 8) % parts for i in turned)


def spread_kernel(order, kv_ref, out_ref, stage, sems):
    parts, _, wide = out_ref.shape
    step = kv_ref.shape[1] // parts
    copies = []
    for c, part in enumerate(order):
        first = part * step - (wide - step)
        if first < 0:
            stage[c, :, : wide - step] = jnp.zeros((ROWS, wide - step), jnp.bfloat16)
            stage[c, :, wide - step :] = kv_ref[:, :step]
        else:
            stage[c] = kv_ref[:, first : first + wide]
        copies.append(pltpu.make_async_copy(stage.at[c], out_ref.at[c], sems.at[c]))
        copies[-1].start()
    for copy in copies:
        copy.wait()


def window_kernel(in_ref, out_ref):
    rows = in_ref.shape[0] * in_ref.shape[1]
    data = in_ref[...].reshape(rows, in_ref.shape[2])
    for j, w in enumerate(PLACES):
        first = 32 * w + 32
        out_ref[j] = data[:, first : first + LANES]


def attend_kernel(order, q_ref, kv_ref, sink_ref, value_ref, out_ref):
    chars = q_ref.shape[1]
    block = lax.axis_index("seq")
    char = lax.broadcasted_iota(jnp.int32, (LANES, chars), 1)
    slot = lax.broadcasted_iota(jnp.int32, (LANES, chars), 0)
    lag = char - SHORT * slot + (SHORT * BACK * 32 - (SHORT - 1))
    visible = (lag >= 0) & (lag < SHORT * BACK * 32) & (slot >= (BACK - block) * 32)
    hidden = jnp.where(visible, jnp.float32(0.0), jnp.float32(-1e30))
    zero = jnp.zeros((HD, chars), jnp.bfloat16)

    def pair(plane):
        first = order.index(plane // FOLD) * ROWS
        slots = [PLACES.index(plane % FOLD * PLANE + w) for w in range(PLANE)]
        return jnp.concatenate([kv_ref[s, first : first + ROWS, :] for s in slots], axis=0)

    for m in range(NH // 2):
        rows = slice(m * LANES, (m + 1) * LANES)
        query = q_ref[rows, :]
        query = jnp.concatenate(
            [
                jnp.concatenate([query[:HD], zero], axis=0),
                jnp.concatenate([zero, query[HD:]], axis=0),
            ],
            axis=1,
        )
        scores = lax.dot_general(
            pair(m), query, (((0,), (0,)), ((), ())), preferred_element_type=jnp.float32
        )
        weights, sinks = [], []
        for side in range(2):
            score = scores[:, side * chars : (side + 1) * chars] * 0.125 + hidden
            sink = sink_ref[2 * m + side : 2 * m + side + 1, :]
            top = jnp.maximum(jnp.max(score, axis=0, keepdims=True), sink)
            expo = jnp.exp(score - top)
            sink_expo = jnp.exp(sink - top)
            inverse = 1.0 / (jnp.sum(expo, axis=0, keepdims=True) + sink_expo)
            weights.append((expo * inverse).astype(jnp.bfloat16))
            sinks.append((sink_expo * inverse).astype(jnp.bfloat16).astype(jnp.float32))
        mixed = jnp.dot(
            pair(m + NH // 2),
            jnp.concatenate(weights, axis=1),
            preferred_element_type=jnp.float32,
        )
        value = value_ref[rows, :]
        even = mixed[:HD, :chars] + sinks[0] * value[:HD]
        odd = mixed[HD:, chars:] + sinks[1] * value[HD:]
        mixed = jnp.concatenate([even, odd], axis=0)
        out_ref[:, rows] = mixed.T.astype(jnp.bfloat16)


def shards(skip_rows, molecule_kv, norm_gain, sink_kv, w_query):
    seq = lax.axis_size("seq")
    sections = lax.axis_size("section")
    planes = seq // PLANE
    order = part_order(planes // FOLD)
    parts = planes // FOLD
    stride = FOLD * PLANE
    columns = [[z * stride + w for z in order] for w in range(stride)]
    rows = [[z * stride + w for w in PLACES] for z in range(parts)]
    width = molecule_kv.shape[2] // parts

    arrived = lax.ppermute(
        molecule_kv, "section", [((i - 1) % sections, i) for i in range(sections)]
    )[0]
    values = skip_rows[0].astype(jnp.float32)
    inverse = lax.rsqrt(jnp.mean(values * values, axis=-1, keepdims=True) + 1e-06)
    chars = values.shape[0]
    sink_value = jnp.broadcast_to(sink_kv[HQ:, None], (HQ, chars))
    arrived, inverse, sink_value = lax.optimization_barrier((arrived, inverse, sink_value))
    normed = (values * inverse * norm_gain).astype(jnp.bfloat16)
    query = jnp.dot(normed, w_query, preferred_element_type=jnp.float32).astype(jnp.bfloat16)
    turned = query.T
    sink = turned.astype(jnp.float32).reshape(NH, HD, chars) * sink_kv[:HQ].reshape(NH, HD, 1)
    sink = jnp.sum(sink, axis=1) * 0.125

    chunks = pl.pallas_call(
        functools.partial(spread_kernel, order),
        out_shape=jax.ShapeDtypeStruct((parts, ROWS, width + LANES), jnp.bfloat16),
        in_specs=[VMEM],
        out_specs=ANY,
        scratch_shapes=[
            pltpu.VMEM((parts, ROWS, width + LANES), jnp.bfloat16),
            pltpu.SemaphoreType.DMA((parts,)),
        ],
        compiler_params=SMALL,
    )(arrived)
    chunks = lax.all_to_all(chunks, "seq", 0, 0, axis_index_groups=columns, tiled=True)
    chunks, turned, sink = lax.optimization_barrier((chunks, turned, sink))
    windows = pl.pallas_call(
        window_kernel,
        out_shape=jax.ShapeDtypeStruct((stride, parts * ROWS, LANES), jnp.bfloat16),
        in_specs=[VMEM],
        out_specs=VMEM,
        compiler_params=SMALL,
    )(chunks)
    keyval = lax.all_to_all(windows, "seq", 0, 0, axis_index_groups=rows, tiled=True)
    mixed = pl.pallas_call(
        functools.partial(attend_kernel, order),
        out_shape=jax.ShapeDtypeStruct((chars, HQ), jnp.bfloat16),
        in_specs=[VMEM] * 4,
        out_specs=VMEM,
        compiler_params=SMALL,
    )(turned, keyval, sink, sink_value)
    return mixed[None]


def solution(mesh):
    return jax.shard_map(
        shards,
        mesh=mesh,
        in_specs=(P("section", "seq", None), P("section", "seq", None), P(), P(), P()),
        out_specs=P("section", "seq", None),
        check_vma=False,
    )
```
